512 devices in a mesh: ctx: 64 (over y, x, z_hi), head: 8 (over z_lo, core).
Axes of the slice: x: 4, y: 4, z: 16 (z_hi: 4, z_lo: 4; z = z_hi * 4 + z_lo), core: 2. Of those that a mesh axis runs over, the one named last changes fastest.
Arguments:
- inputs: bfloat16 [8192, 2304], P('ctx', 'head'), may hold values from -0.15625 to 0.15625
- queries: bfloat16 [8192, 2048], P('ctx', 'head'), may hold values from -18 to 18
- keys: bfloat16 [8192, 1024], P('ctx', 'head'), may hold values from -6 to 6
- values: bfloat16 [8192, 1024], P('ctx', 'head'), may hold values from -6 to 6
- grad_out: bfloat16 [8192, 2048], P('ctx', 'head'), may hold values from -6 to 6
- w_query: bfloat16 [2304, 2048], P(None, 'head'), may hold values from -0.125 to 0.125
- w_key: bfloat16 [2304, 1024], P(None, 'head'), may hold values from -0.1875 to 0.1875
- w_value: bfloat16 [2304, 1024], P(None, 'head'), may hold values from -0.1875 to 0.1875
- doc_lengths: int32 [17], replicated, may hold values from 1 to 3072, 8192 in all
Outputs:
- grad_input: bfloat16 [8192, 2304], P('ctx', 'head')
- grad_key_weight: float32 [2304, 1024], P('ctx', 'head')
- grad_value_weight: float32 [2304, 1024], P('ctx', 'head')
The draws below stay inside these ranges and needn't reach their ends.
Inputs may be any that keep to these rules, and one draw needn't show every extreme that they name: `doc_lengths`: the 17 lengths sum to 8192, and the longest is exactly 3072.
All inputs are finite; a program needn't handle non-finite values.
Results may differ from the reference program's by a relative error of at most 0.017.
Values may be sent and summed in bfloat16 or wider, within the bound.
No kernel may reach another device: no remote copies, remote signals or barrier semaphores. Data moves between devices by JAX's collectives and lax.ppermute only.
A program may use at most 64 MiB of HBM per device.

```python
import math
import jax
import jax.numpy as jnp
import numpy as np
from jax import lax

D = 2304
HEAD_DIM = 128
QH_DEV = 2
HEADS = 16
KV_HEADS = 8
SEQ = 8192
MOST = 3072
NDOCS = 17


def strengthened(entries, stream_key, source, target, shards_of, factor):
    owner, partner = [(jnp.arange(entries.shape[axis_at]) // (entries.shape[axis_at] // shards_of)).reshape([-1 if axis == axis_at else 1 for axis in range(entries.ndim)]) for axis_at in (source, target)]
    chosen = jax.random.permutation(stream_key, shards_of)[partner]
    strong = (owner == chosen) | (owner == (partner + shards_of // 2) % shards_of)
    return jnp.where(strong, factor * entries, entries)


def shard_levels(rng, extent, cuts, smallest, top_value):
    loudness, own = 1.0, jax.random.fold_in(rng, 6)
    for position, parts in cuts:
        steps = jnp.exp(jax.random.uniform(jax.random.fold_in(own, position), (parts,), jnp.float32, smallest / len(cuts), top_value / len(cuts)))
        loudness = loudness * jnp.repeat(steps, extent[position] // parts).reshape([-1 if axis == position else 1 for axis in range(len(extent))])
    return loudness


def split_up(amount, total, limit, lean):
    portions = [(1 << 20) // math.isqrt(standing ** lean) + 1 for standing in range(2, amount + 1)]
    spare, given = total - limit - (amount - 1), [1] * (amount - 1)
    while spare > 0:
        movable = [i for i in range(amount - 1) if given[i] < limit]
        mass, remaining = sum([portions[i] for i in movable]), spare
        for i in movable:
            more = min(limit - given[i], max(1, remaining * portions[i] // mass), spare)
            given[i] = given[i] + more
            spare = spare - more
    return np.array([limit] + given)


def ragged(rng, amount, total, reach, lean):
    if amount == 2:
        one = jax.random.randint(rng, (), max(1, total - reach), min(reach, total - 1) + 1)
        return jnp.stack([one, total - one])
    sizes = jnp.asarray(split_up(amount, total, reach, lean), jnp.int32)
    couples = (amount - 1) // 2
    source_of, sink = sizes[1:1 + 2 * couples:2], sizes[2:2 + 2 * couples:2]
    room = jnp.minimum(source_of - 1, reach - sink)
    passed = jax.random.randint(jax.random.fold_in(rng, 1), (couples,), 0, 1 << 20) % (room + 1)
    sizes = sizes.at[1:1 + 2 * couples:2].set(source_of - passed).at[2:2 + 2 * couples:2].set(sink + passed)
    return sizes[jax.random.permutation(jax.random.fold_in(rng, 2), amount)]


def centred(rng, dims, width, reach, split=(), kind=jnp.bfloat16):
    factor_of = shard_levels(rng, dims, split, -0.22, 0.18) if split else 1.0
    result = jax.random.normal(rng, dims, jnp.float32) * width * factor_of
    return jnp.minimum(jnp.maximum(result, -reach), reach).astype(kind)


def bell_draw_with(key, shape, deviation, limit, pieces, heavy, kind=jnp.bfloat16):
    entries = deviation * jax.random.normal(key, shape, jnp.float32)
    if pieces:
        entries = entries * shard_levels(key, shape, pieces, -0.22, 0.18)
    return jnp.clip(strengthened(entries, jax.random.fold_in(key, 3), *heavy), -limit, limit).astype(kind)


def setup_inputs(seed: int = 0) -> dict:
    streams_of = jax.random.split(jax.random.key(seed), 10)
    return {
        "inputs": bell_draw_with(streams_of[0], (SEQ, D), 0.01, 0.15625, ((0, 64), (1, 8)), (0, 1, 64, 4.0)),
        "queries": centred(streams_of[1], (SEQ, HEADS * HEAD_DIM), 3.0, 18.0, ((0, 64), (1, 8))),
        "keys": centred(streams_of[2], (SEQ, KV_HEADS * HEAD_DIM), 1.0, 6.0, ((0, 64), (1, 8))),
        "values": centred(streams_of[3], (SEQ, KV_HEADS * HEAD_DIM), 1.0, 6.0, ((0, 64), (1, 8))),
        "grad_out": centred(streams_of[4], (SEQ, HEADS * HEAD_DIM), 1.0, 6.0, ((0, 64), (1, 8))),
        "w_query": centred(streams_of[5], (D, HEADS * HEAD_DIM), (HEADS * HEAD_DIM) ** -0.5, 0.125, ((1, 8),)),
        "w_key": centred(streams_of[6], (D, KV_HEADS * HEAD_DIM), (KV_HEADS * HEAD_DIM) ** -0.5, 0.1875, ((1, 8),)),
        "w_value": centred(streams_of[7], (D, KV_HEADS * HEAD_DIM), (KV_HEADS * HEAD_DIM) ** -0.5, 0.1875, ((1, 8),)),
        "doc_lengths": ragged(streams_of[8], NDOCS, SEQ, MOST, 2).astype(jnp.int32),
    }


QUERY_SCALE = 1.0 / 12.0
SOFT_CAP = 50.0


def head_grads(operands, doc_seg, positions):
    query_head, key_head, value_head, grad_head = operands
    block_rows = min(512, SEQ)

    def step(carry_state, block_index):
        grad_key, grad_value = carry_state
        start_row = block_index * block_rows
        query_block = lax.dynamic_slice_in_dim(query_head, start_row, block_rows, 0)
        grad_block = lax.dynamic_slice_in_dim(grad_head, start_row, block_rows, 0)
        query_pos = lax.dynamic_slice_in_dim(positions, start_row, block_rows, 0)
        query_seg = lax.dynamic_slice_in_dim(doc_seg, start_row, block_rows, 0)
        allowed = (query_seg[:, None] == doc_seg[None, :]) & (positions[None, :] <= query_pos[:, None])
        raw = jnp.dot(query_block, key_head.T, preferred_element_type=jnp.float32) * QUERY_SCALE
        scores = SOFT_CAP * jnp.tanh(raw / SOFT_CAP)
        weights = jnp.where(allowed, jnp.exp(scores), 0.0)
        totals = jnp.sum(weights, axis=-1)
        mixed = jnp.dot(weights.astype(jnp.bfloat16), value_head, preferred_element_type=jnp.float32) / totals[:, None]
        deltas = jnp.sum(grad_block.astype(jnp.float32) * mixed, axis=-1)
        probs = weights / totals[:, None]
        grad_prob = jnp.dot(grad_block, value_head.T, preferred_element_type=jnp.float32)
        slope = (QUERY_SCALE * probs * (grad_prob - deltas[:, None]) * (1.0 - (scores / SOFT_CAP) ** 2)).astype(jnp.bfloat16)
        grad_query = jnp.dot(slope, key_head, preferred_element_type=jnp.float32)
        grad_key = grad_key + jnp.dot(slope.T, query_block, preferred_element_type=jnp.float32)
        grad_value = grad_value + jnp.dot(probs.astype(jnp.bfloat16).T, grad_block, preferred_element_type=jnp.float32)
        return (grad_key, grad_value), grad_query

    empty = jnp.zeros((SEQ, HEAD_DIM), jnp.float32)
    block_count = SEQ // block_rows
    (grad_key, grad_value), grad_query = lax.scan(step, (empty, empty), jnp.arange(block_count, dtype=jnp.int32))
    return grad_query.reshape(SEQ, HEAD_DIM), grad_key, grad_value


def reference(inputs, queries, keys, values, grad_out, w_query, w_key, w_value, doc_lengths):
    positions = jnp.arange(SEQ, dtype=jnp.int32)
    doc_ends = jnp.cumsum(doc_lengths).astype(jnp.int32)
    doc_seg = jnp.sum((doc_ends[None, :] <= positions[:, None]).astype(jnp.int32), axis=1)
    query_heads = queries.reshape(SEQ, HEADS, HEAD_DIM).transpose(1, 0, 2)
    grad_heads = grad_out.reshape(SEQ, HEADS, HEAD_DIM).transpose(1, 0, 2)
    key_heads = jnp.repeat(keys.reshape(SEQ, KV_HEADS, HEAD_DIM).transpose(1, 0, 2), QH_DEV, axis=0)
    value_heads = jnp.repeat(values.reshape(SEQ, KV_HEADS, HEAD_DIM).transpose(1, 0, 2), QH_DEV, axis=0)
    grad_query, grad_key, grad_value = lax.map(
        lambda operands: head_grads(operands, doc_seg, positions),
        (query_heads, key_heads, value_heads, grad_heads))
    grad_query = grad_query.astype(jnp.bfloat16).transpose(1, 0, 2).reshape(SEQ, HEADS * HEAD_DIM)
    grad_key = grad_key.reshape(KV_HEADS, QH_DEV, SEQ, HEAD_DIM).sum(axis=1).astype(jnp.bfloat16)
    grad_key = grad_key.transpose(1, 0, 2).reshape(SEQ, KV_HEADS * HEAD_DIM)
    grad_value = grad_value.reshape(KV_HEADS, QH_DEV, SEQ, HEAD_DIM).sum(axis=1).astype(jnp.bfloat16)
    grad_value = grad_value.transpose(1, 0, 2).reshape(SEQ, KV_HEADS * HEAD_DIM)
    query_cols = QH_DEV * HEAD_DIM
    grad_input = jnp.zeros((SEQ, D), jnp.float32)
    for group_index in range(KV_HEADS):
        query_start = group_index * query_cols
        key_start = group_index * HEAD_DIM
        group_term = jnp.dot(grad_query[:, query_start:query_start + query_cols],
                             w_query[:, query_start:query_start + query_cols].T,
                             preferred_element_type=jnp.float32)
        group_term = group_term + jnp.dot(grad_key[:, key_start:key_start + HEAD_DIM],
                                          w_key[:, key_start:key_start + HEAD_DIM].T,
                                          preferred_element_type=jnp.float32)
        group_term = group_term + jnp.dot(grad_value[:, key_start:key_start + HEAD_DIM],
                                          w_value[:, key_start:key_start + HEAD_DIM].T,
                                          preferred_element_type=jnp.float32)
        grad_input = grad_input + lax.optimization_barrier(group_term.astype(jnp.bfloat16)).astype(jnp.float32)
    grad_key_weight = jnp.dot(inputs.T, grad_key, preferred_element_type=jnp.float32)
    grad_value_weight = jnp.dot(inputs.T, grad_value, preferred_element_type=jnp.float32)
    return grad_input.astype(jnp.bfloat16), grad_key_weight, grad_value_weight
```

```python
import jax
import jax.numpy as jnp
from jax import lax
from jax.experimental import pallas as pl
from jax.experimental.pallas import tpu as pltpu
from jax.sharding import Mesh, PartitionSpec as P

QUERY_SCALE = 1.0 / 12.0
SOFT_CAP = 50.0
PLANE = ("y", "x")
LINES = ("zh", "zl")
CHUNK = 128
WIDTH = 128
GROUP = 4
BLOCKS = 16
SPAN = GROUP * CHUNK
NT = (((1,), (1,)), ((), ()))
TN = (((0,), (0,)), ((), ()))
NN = (((1,), (0,)), ((), ()))
F32 = jnp.float32
BF16 = jnp.bfloat16


def dot(left, right, dims):
    return lax.dot_general(left, right, dims, preferred_element_type=F32)


def swapped(value):
    return lax.ppermute(value, LINES, [(a * 4 + b, b * 4 + a) for a in range(4) for b in range(4)])


def partner(value, axis, mask):
    return lax.ppermute(value, axis, [(i, i ^ mask) for i in range(lax.axis_size(axis))])


def gathered(value, axis):
    return [value] + [partner(value, axis, mask) for mask in (1, 2, 3)]


def returned(parts, axis):
    return [parts[0]] + [partner(parts[mask], axis, mask) for mask in (1, 2, 3)]


def exchange(parts, axes):
    return lax.all_to_all(parts, axes, 0, 0, tiled=True)


def spread(value, count, axes):
    return exchange(jnp.broadcast_to(value[None], (count,) + value.shape), axes)


def added(parts):
    return jnp.sum(parts.astype(F32), axis=0)


def query_bounds(place_ref, lengths_ref):
    block, own = place_ref[0], place_ref[1]
    first = block * SPAN
    lane = lax.broadcasted_iota(jnp.int32, (1, CHUNK), 1)
    pos = jnp.concatenate([first + (own ^ slot) * CHUNK + lane for slot in range(GROUP)], axis=1)
    start = jnp.zeros((1, SPAN), jnp.int32)
    end = jnp.int32(0)
    earliest = jnp.int32(0)
    for doc in range(lengths_ref.shape[0]):
        end = end + lengths_ref[doc]
        start = jnp.where(pos >= end, end, start)
        earliest = jnp.where(end <= first, end, earliest)
    return start, pos, lax.div(earliest, SPAN), block + 1


def join_rows(slots, rows_ref):
    for slot in range(GROUP):
        rows_ref[slot * CHUNK:(slot + 1) * CHUNK, :] = slots[slot][...]


def allowed_pairs(place_ref, block, start, pos):
    key_pos = block * SPAN + place_ref[1] * CHUNK + lax.broadcasted_iota(jnp.int32, (CHUNK, SPAN), 0)
    return (key_pos >= start) & (key_pos <= pos)


def weighted(key_rows, query, allowed):
    capped = jnp.tanh(dot(key_rows, query, NT) * (QUERY_SCALE / SOFT_CAP))
    return capped, jnp.where(allowed, jnp.exp(SOFT_CAP * capped), 0.0)


def stats_kernel(place_ref, lengths_ref, kv_ref, slot0, slot1, slot2, slot3, stats_ref, rows_ref):
    join_rows((slot0, slot1, slot2, slot3), rows_ref)
    start, pos, low, high = query_bounds(place_ref, lengths_ref)

    def step(block, carry):
        key_rows = kv_ref[block, :, :WIDTH]
        value_rows = kv_ref[block, :, WIDTH:]
        allowed = allowed_pairs(place_ref, block, start, pos)
        result = []
        for head in range(2):
            query = rows_ref[:, head * WIDTH:(head + 1) * WIDTH]
            grad = rows_ref[:, (2 + head) * WIDTH:(3 + head) * WIDTH]
            _, weights = weighted(key_rows, query, allowed)
            grad_prob = dot(value_rows, grad, NT)
            result.append(carry[2 * head] + jnp.sum(weights, axis=0, keepdims=True))
            result.append(carry[2 * head + 1] + jnp.sum(weights * grad_prob, axis=0, keepdims=True))
        return tuple(result)

    empty = jnp.zeros((1, SPAN), F32)
    totals = lax.fori_loop(low, high, step, (empty,) * 4)
    stats_ref[...] = jnp.concatenate(totals, axis=0)


def grads_kernel(
    place_ref, lengths_ref, stats_ref, kv_ref, slot0, slot1, slot2, slot3, query_ref, kv_out_ref, rows_ref, sums_ref
):
    join_rows((slot0, slot1, slot2, slot3), rows_ref)
    start, pos, low, high = query_bounds(place_ref, lengths_ref)
    own = place_ref[1]
    lanes = [stats_ref[own ^ lane] for lane in range(GROUP)]
    stats = jnp.concatenate(
        [
            sum(lanes[lane][:, (slot ^ lane) * CHUNK:((slot ^ lane) + 1) * CHUNK] for lane in range(GROUP))
            for slot in range(GROUP)
        ],
        axis=1,
    )
    inverse = [1.0 / stats[2 * head:2 * head + 1] for head in range(2)]
    deltas = [stats[2 * head + 1:2 * head + 2] * inverse[head] for head in range(2)]
    sums_ref[...] = jnp.zeros_like(sums_ref)
    kv_out_ref[...] = jnp.zeros_like(kv_out_ref)

    def step(block, carry):
        key_rows = kv_ref[block, :, :WIDTH]
        value_rows = kv_ref[block, :, WIDTH:]
        allowed = allowed_pairs(place_ref, block, start, pos)
        key_sum = jnp.zeros((CHUNK, WIDTH), F32)
        value_sum = jnp.zeros((CHUNK, WIDTH), F32)
        for head in range(2):
            query = rows_ref[:, head * WIDTH:(head + 1) * WIDTH]
            grad = rows_ref[:, (2 + head) * WIDTH:(3 + head) * WIDTH]
            capped, weights = weighted(key_rows, query, allowed)
            probs = weights * inverse[head]
            grad_prob = dot(value_rows, grad, NT)
            slope = (probs * QUERY_SCALE * (grad_prob - deltas[head]) * (1.0 - capped * capped)).astype(BF16)
            key_sum = key_sum + dot(slope, query, NN)
            value_sum = value_sum + dot(probs.astype(BF16), grad, NN)
            sums_ref[head * WIDTH:(head + 1) * WIDTH, :] += dot(key_rows, slope, TN)
        kv_out_ref[block] = jnp.concatenate([key_sum, value_sum], axis=1).astype(BF16)
        return carry

    lax.fori_loop(low, high, step, 0)
    for slot in range(GROUP):
        query_ref[slot] = sums_ref[:, slot * CHUNK:(slot + 1) * CHUNK].astype(BF16)


def term_kernel(place_ref, wq_ref, wk_ref, wv_ref, query_ref, kv_ref, out_ref):
    rows = wq_ref.shape[0] // 8
    key_part = kv_ref[:, :WIDTH].T
    value_part = kv_ref[:, WIDTH:].T
    for side in range(2):
        for line in range(GROUP):
            block = pl.ds(pl.multiple_of(((place_ref[1] ^ line) * 2 + (place_ref[3] ^ (1 - side))) * rows, 32), rows)
            total = dot(wq_ref[block, :], query_ref[...], NN)
            total = total + dot(wk_ref[block, :], key_part, NN)
            total = total + dot(wv_ref[block, :], value_part, NN)
            out_ref[side, line] = total.astype(BF16)


def run_kernel(body, shapes, scratch, flops, scalars, operands):
    smem = pl.BlockSpec(memory_space=pltpu.SMEM)
    vmem = pl.BlockSpec(memory_space=pltpu.VMEM)
    return pl.pallas_call(
        body,
        out_shape=shapes,
        in_specs=[smem] * len(scalars) + [vmem] * len(operands),
        out_specs=jax.tree.map(lambda _: vmem, shapes),
        scratch_shapes=scratch,
        compiler_params=pltpu.CompilerParams(vmem_limit_bytes=40 * 1024 * 1024),
        cost_estimate=pl.CostEstimate(flops=flops, bytes_accessed=4000000, transcendentals=2000000),
    )(*scalars, *operands)


def shards(inputs, queries, keys, values, grad_out, w_query, w_key, w_value, doc_lengths):
    zh, zl, core = lax.axis_index("zh"), lax.axis_index("zl"), lax.axis_index("c")
    place = jnp.stack([lax.axis_index(PLANE), zl, zh, core]).astype(jnp.int32)
    lengths = doc_lengths.astype(jnp.int32)

    packed = swapped(jnp.concatenate([keys, values, queries, grad_out], axis=1))
    features = lax.all_gather(inputs.T, ("zl", "c"), axis=0, tiled=True)
    packed, features = lax.optimization_barrier((packed, features))
    kv_all = spread(packed[:, :2 * WIDTH], BLOCKS, PLANE)
    rows = gathered(packed[:, 2 * WIDTH:], "zl")
    joined = pltpu.VMEM((SPAN, 4 * WIDTH), BF16)
    stats = run_kernel(
        stats_kernel, jax.ShapeDtypeStruct((4, SPAN), F32), [joined], 500000000, (place, lengths), (kv_all, *rows)
    )
    stats_all = spread(stats, GROUP, "zl")
    query_parts, kv_parts = run_kernel(
        grads_kernel,
        (jax.ShapeDtypeStruct((GROUP, 2 * WIDTH, CHUNK), BF16), jax.ShapeDtypeStruct((BLOCKS, CHUNK, 2 * WIDTH), BF16)),
        [joined, pltpu.VMEM((2 * WIDTH, SPAN), F32)],
        1200000000,
        (place, lengths),
        (stats_all, kv_all, *rows),
    )
    kv_parts = exchange(kv_parts, PLANE)
    query_parts = returned([query_parts[slot] for slot in range(GROUP)], "zl")
    grad_query = swapped(sum(part.astype(F32) for part in query_parts).astype(BF16))
    grad_kv = added(kv_parts).astype(BF16)

    grad_kv = swapped(grad_kv)

    weight = dot(features, grad_kv, NN).astype(BF16).reshape(BLOCKS, -1, 2 * WIDTH)
    weight = added(exchange(weight, PLANE)).astype(BF16).reshape(GROUP, -1, 2 * WIDTH)
    weight = added(exchange(weight, "zh"))

    side = jax.ShapeDtypeStruct((2, GROUP, w_query.shape[0] // 8, CHUNK), BF16)
    terms = run_kernel(term_kernel, side, [], 300000000, (place,), (w_query, w_key, w_value, grad_query, grad_kv))
    both = (terms[1].astype(F32) + partner(terms[0], "c", 1).astype(F32)).astype(BF16)
    pieces = returned([both[slot] for slot in range(GROUP)], "zl")
    grad_input = sum(piece.astype(F32) for piece in pieces).T.astype(BF16)
    return grad_input, weight[:, :WIDTH], weight[:, WIDTH:]


def solution(mesh):
    fine = Mesh(mesh.devices.reshape(4, 4, 4, 4, 2), ("y", "x", "zh", "zl", "c"))
    ctx, head = ("y", "x", "zh"), ("zl", "c")
    split = P(ctx, head)
    return jax.shard_map(
        shards,
        mesh=fine,
        in_specs=(split,) * 5 + (P(None, head),) * 3 + (P(),),
        out_specs=(split,) * 3,
        check_vma=False,
    )
```

```python
import jax
import jax.numpy as jnp
from jax import lax
from jax.experimental import pallas as pl
from jax.experimental.pallas import tpu as pltpu
from jax.sharding import Mesh, PartitionSpec as P

QUERY_SCALE = 1.0 / 12.0
SOFT_CAP = 50.0
PLANE = ("y", "x")
LINES = ("zh", "zl")
CHUNK = 128
WIDTH = 128
GROUP = 4
BLOCKS = 16
SPAN = GROUP * CHUNK
PAIR = 2
TILE = 256
NT = (((1,), (1,)), ((), ()))
TN = (((0,), (0,)), ((), ()))
NN = (((1,), (0,)), ((), ()))
F32 = jnp.float32
BF16 = jnp.bfloat16


def dot(left, right, dims):
    return lax.dot_general(left, right, dims, preferred_element_type=F32)


def swapped(value):
    return lax.ppermute(value, LINES, [(a * 4 + b, b * 4 + a) for a in range(4) for b in range(4)])


def partner(value, axis, mask):
    return lax.ppermute(value, axis, [(i, i ^ mask) for i in range(lax.axis_size(axis))])


def gathered(value, axis):
    return [value] + [partner(value, axis, mask) for mask in (1, 2, 3)]


def returned(parts, axis):
    return [parts[0]] + [partner(parts[mask], axis, mask) for mask in (1, 2, 3)]


def exchange(parts, axes):
    return lax.all_to_all(parts, axes, 0, 0, tiled=True)


def spread(value, count, axes):
    return exchange(jnp.broadcast_to(value[None], (count,) + value.shape), axes)


def added(parts):
    return jnp.sum(parts.astype(F32), axis=0)


def query_bounds(place_ref, lengths_ref):
    block, own = place_ref[0], place_ref[1]
    first = block * SPAN
    lane = lax.broadcasted_iota(jnp.int32, (1, CHUNK), 1)
    pos = jnp.concatenate([first + (own ^ slot) * CHUNK + lane for slot in range(GROUP)], axis=1)
    start = jnp.zeros((1, SPAN), jnp.int32)
    end = jnp.int32(0)
    earliest = jnp.int32(0)
    for doc in range(lengths_ref.shape[0]):
        end = end + lengths_ref[doc]
        start = jnp.where(pos >= end, end, start)
        earliest = jnp.where(end <= first, end, earliest)
    return start, pos, lax.div(earliest, PAIR * SPAN), lax.div(block, PAIR) + 1


def join_rows(slots, rows_ref):
    for slot in range(GROUP):
        rows_ref[slot * CHUNK:(slot + 1) * CHUNK, :] = slots[slot][...]


def allowed_pairs(place_ref, block, start, pos):
    row = lax.broadcasted_iota(jnp.int32, (PAIR * CHUNK, TILE), 0)
    key_pos = (block * PAIR) * SPAN + place_ref[1] * CHUNK + row + jnp.where(row >= CHUNK, SPAN - CHUNK, 0)
    return (key_pos >= start) & (key_pos <= pos)


def weighted(key_rows, query, allowed):
    capped = jnp.tanh(dot(key_rows, query, NT) * (QUERY_SCALE / SOFT_CAP))
    return capped, jnp.where(allowed, jnp.exp(SOFT_CAP * capped), 0.0)


def stats_kernel(place_ref, lengths_ref, kv_ref, slot0, slot1, slot2, slot3, stats_ref, rows_ref):
    join_rows((slot0, slot1, slot2, slot3), rows_ref)
    start, pos, low, high = query_bounds(place_ref, lengths_ref)

    def step(block, carry):
        kv_rows = kv_ref[pl.ds(block * PAIR, PAIR)].reshape(PAIR * CHUNK, 2 * WIDTH)
        sums = [[] for _ in range(4)]
        for first in range(0, SPAN, TILE):
            part = slice(first, first + TILE)
            allowed = allowed_pairs(place_ref, block, start[:, part], pos[:, part])
            for head in range(2):
                query = rows_ref[part, head * WIDTH:(head + 1) * WIDTH]
                grad = rows_ref[part, (2 + head) * WIDTH:(3 + head) * WIDTH]
                _, weights = weighted(kv_rows[:, :WIDTH], query, allowed)
                grad_prob = dot(kv_rows[:, WIDTH:], grad, NT)
                sums[2 * head].append(jnp.sum(weights, axis=0, keepdims=True))
                sums[2 * head + 1].append(jnp.sum(weights * grad_prob, axis=0, keepdims=True))
        return tuple(total + jnp.concatenate(parts, axis=1) for total, parts in zip(carry, sums))

    empty = jnp.zeros((1, SPAN), F32)
    totals = lax.fori_loop(low, high, step, (empty,) * 4)
    stats_ref[...] = jnp.concatenate(totals, axis=0)


def grads_kernel(
    place_ref, lengths_ref, stats_ref, kv_ref, slot0, slot1, slot2, slot3, query_ref, kv_out_ref, rows_ref, sums_ref
):
    join_rows((slot0, slot1, slot2, slot3), rows_ref)
    start, pos, low, high = query_bounds(place_ref, lengths_ref)
    own = place_ref[1]
    lanes = [stats_ref[own ^ lane] for lane in range(GROUP)]
    stats = jnp.concatenate(
        [
            sum(lanes[lane][:, (slot ^ lane) * CHUNK:((slot ^ lane) + 1) * CHUNK] for lane in range(GROUP))
            for slot in range(GROUP)
        ],
        axis=1,
    )
    inverse = [1.0 / stats[2 * head:2 * head + 1] for head in range(2)]
    deltas = [stats[2 * head + 1:2 * head + 2] * inverse[head] for head in range(2)]
    sums_ref[...] = jnp.zeros_like(sums_ref)
    kv_out_ref[...] = jnp.zeros_like(kv_out_ref)

    def step(block, carry):
        kv_rows = kv_ref[pl.ds(block * PAIR, PAIR)].reshape(PAIR * CHUNK, 2 * WIDTH)
        key_rows = kv_rows[:, :WIDTH]
        key_sum = jnp.zeros((PAIR * CHUNK, WIDTH), F32)
        value_sum = jnp.zeros((PAIR * CHUNK, WIDTH), F32)
        for first in range(0, SPAN, TILE):
            part = slice(first, first + TILE)
            allowed = allowed_pairs(place_ref, block, start[:, part], pos[:, part])
            for head in range(2):
                query = rows_ref[part, head * WIDTH:(head + 1) * WIDTH]
                grad = rows_ref[part, (2 + head) * WIDTH:(3 + head) * WIDTH]
                capped, weights = weighted(key_rows, query, allowed)
                probs = weights * inverse[head][:, part]
                grad_prob = dot(kv_rows[:, WIDTH:], grad, NT)
                slope = probs * (grad_prob - deltas[head][:, part]) * (QUERY_SCALE - QUERY_SCALE * capped * capped)
                slope = slope.astype(BF16)
                key_sum = key_sum + dot(slope, query, NN)
                value_sum = value_sum + dot(probs.astype(BF16), grad, NN)
                sums_ref[head * WIDTH:(head + 1) * WIDTH, part] += dot(key_rows, slope, TN)
        result = jnp.concatenate([key_sum, value_sum], axis=1).astype(BF16)
        kv_out_ref[pl.ds(block * PAIR, PAIR)] = result.reshape(PAIR, CHUNK, 2 * WIDTH)
        return carry

    lax.fori_loop(low, high, step, 0)
    for slot in range(GROUP):
        query_ref[slot] = sums_ref[:, slot * CHUNK:(slot + 1) * CHUNK].astype(BF16)


def term_kernel(place_ref, wq_ref, wk_ref, wv_ref, query_ref, kv_ref, out_ref):
    rows = wq_ref.shape[0] // 8
    key_part = kv_ref[:, :WIDTH].T
    value_part = kv_ref[:, WIDTH:].T
    for side in range(2):
        for line in range(GROUP):
            block = pl.ds(pl.multiple_of(((place_ref[1] ^ line) * 2 + (place_ref[3] ^ (1 - side))) * rows, 32), rows)
            total = dot(wq_ref[block, :], query_ref[...], NN)
            total = total + dot(wk_ref[block, :], key_part, NN)
            total = total + dot(wv_ref[block, :], value_part, NN)
            out_ref[side, line] = total.astype(BF16)


def run_kernel(body, shapes, scratch, flops, scalars, operands):
    smem = pl.BlockSpec(memory_space=pltpu.SMEM)
    vmem = pl.BlockSpec(memory_space=pltpu.VMEM)
    return pl.pallas_call(
        body,
        out_shape=shapes,
        in_specs=[smem] * len(scalars) + [vmem] * len(operands),
        out_specs=jax.tree.map(lambda _: vmem, shapes),
        scratch_shapes=scratch,
        compiler_params=pltpu.CompilerParams(vmem_limit_bytes=40 * 1024 * 1024),
        cost_estimate=pl.CostEstimate(flops=flops, bytes_accessed=4000000, transcendentals=2000000),
    )(*scalars, *operands)


def shards(inputs, queries, keys, values, grad_out, w_query, w_key, w_value, doc_lengths):
    zh, zl, core = lax.axis_index("zh"), lax.axis_index("zl"), lax.axis_index("c")
    place = jnp.stack([lax.axis_index(PLANE), zl, zh, core]).astype(jnp.int32)
    lengths = doc_lengths.astype(jnp.int32)

    packed = swapped(jnp.concatenate([keys, values, queries, grad_out], axis=1))
    features = lax.all_gather(inputs.T, ("zl", "c"), axis=0, tiled=True)
    packed, features = lax.optimization_barrier((packed, features))
    kv_all = spread(packed[:, :2 * WIDTH], BLOCKS, PLANE)
    rows = gathered(packed[:, 2 * WIDTH:], "zl")
    joined = pltpu.VMEM((SPAN, 4 * WIDTH), BF16)
    stats = run_kernel(
        stats_kernel, jax.ShapeDtypeStruct((4, SPAN), F32), [joined], 500000000, (place, lengths), (kv_all, *rows)
    )
    stats_all = spread(stats, GROUP, "zl")
    query_parts, kv_parts = run_kernel(
        grads_kernel,
        (jax.ShapeDtypeStruct((GROUP, 2 * WIDTH, CHUNK), BF16), jax.ShapeDtypeStruct((BLOCKS, CHUNK, 2 * WIDTH), BF16)),
        [joined, pltpu.VMEM((2 * WIDTH, SPAN), F32)],
        1200000000,
        (place, lengths),
        (stats_all, kv_all, *rows),
    )
    kv_parts = exchange(kv_parts, PLANE)
    query_parts = returned([query_parts[slot] for slot in range(GROUP)], "zl")
    grad_query = swapped(sum(part.astype(F32) for part in query_parts).astype(BF16))
    grad_kv = added(kv_parts).astype(BF16)

    grad_kv = swapped(grad_kv)

    weight = dot(features, grad_kv, NN).astype(BF16).reshape(BLOCKS, -1, 2 * WIDTH)
    weight = added(exchange(weight, PLANE)).astype(BF16).reshape(GROUP, -1, 2 * WIDTH)
    weight = added(exchange(weight, "zh"))

    side = jax.ShapeDtypeStruct((2, GROUP, w_query.shape[0] // 8, CHUNK), BF16)
    terms = run_kernel(term_kernel, side, [], 300000000, (place,), (w_query, w_key, w_value, grad_query, grad_kv))
    both = (terms[1].astype(F32) + partner(terms[0], "c", 1).astype(F32)).astype(BF16)
    pieces = returned([both[slot] for slot in range(GROUP)], "zl")
    grad_input = sum(piece.astype(F32) for piece in pieces).T.astype(BF16)
    return grad_input, weight[:, :WIDTH], weight[:, WIDTH:]


def solution(mesh):
    fine = Mesh(mesh.devices.reshape(4, 4, 4, 4, 2), ("y", "x", "zh", "zl", "c"))
    ctx, head = ("y", "x", "zh"), ("zl", "c")
    split = P(ctx, head)
    return jax.shard_map(
        shards,
        mesh=fine,
        in_specs=(split,) * 5 + (P(None, head),) * 3 + (P(),),
        out_specs=(split,) * 3,
        check_vma=False,
    )
```

```python
import jax
import jax.numpy as jnp
from jax import lax
from jax.experimental import pallas as pl
from jax.experimental.pallas import tpu as pltpu
from jax.sharding import Mesh, PartitionSpec as P

QUERY_SCALE = 1.0 / 12.0
SOFT_CAP = 50.0
LOG2_E = 1.4426950408889634
PLANE = ("y", "x")
LINES = ("zh", "zl")
CHUNK = 128
WIDTH = 128
GROUP = 4
BLOCKS = 16
SPAN = GROUP * CHUNK
PAIR = 2
TILE = 256
NT = (((1,), (1,)), ((), ()))
TN = (((0,), (0,)), ((), ()))
NN = (((1,), (0,)), ((), ()))
F32 = jnp.float32
BF16 = jnp.bfloat16


def dot(left, right, dims):
    return lax.dot_general(left, right, dims, preferred_element_type=F32)


def swapped(value):
    return lax.ppermute(value, LINES, [(a * 4 + b, b * 4 + a) for a in range(4) for b in range(4)])


def partner(value, axis, mask):
    return lax.ppermute(value, axis, [(i, i ^ mask) for i in range(lax.axis_size(axis))])


def gathered(value, axis):
    return [value] + [partner(value, axis, mask) for mask in (1, 2, 3)]


def returned(parts, axis):
    return [parts[0]] + [partner(parts[mask], axis, mask) for mask in (1, 2, 3)]


def exchange(parts, axes):
    return lax.all_to_all(parts, axes, 0, 0, tiled=True)


def spread(value, count, axes):
    return exchange(jnp.broadcast_to(value[None], (count,) + value.shape), axes)


def added(parts):
    return jnp.sum(parts.astype(F32), axis=0)


def query_bounds(place_ref, lengths_ref):
    block, own = place_ref[0], place_ref[1]
    first = block * SPAN
    lane = lax.broadcasted_iota(jnp.int32, (1, CHUNK), 1)
    pos = jnp.concatenate([first + (own ^ slot) * CHUNK + lane for slot in range(GROUP)], axis=1)
    start = jnp.zeros((1, SPAN), jnp.int32)
    end = jnp.int32(0)
    earliest = jnp.int32(0)
    for doc in range(lengths_ref.shape[0]):
        end = end + lengths_ref[doc]
        start = jnp.where(pos >= end, end, start)
        earliest = jnp.where(end <= first, end, earliest)
    return start, pos, lax.div(earliest, PAIR * SPAN), lax.div(block, PAIR) + 1


def join_rows(slots, rows_ref):
    for slot in range(GROUP):
        rows_ref[slot * CHUNK:(slot + 1) * CHUNK, :] = slots[slot][...]


def allowed_pairs(place_ref, block, start, pos):
    row = lax.broadcasted_iota(jnp.int32, (PAIR * CHUNK, TILE), 0)
    key_pos = (block * PAIR) * SPAN + place_ref[1] * CHUNK + row + jnp.where(row >= CHUNK, SPAN - CHUNK, 0)
    return (key_pos >= start) & (key_pos <= pos)


def weighted(key_rows, query, allowed):
    capped = jnp.tanh(dot(key_rows, query, NT) * (QUERY_SCALE / SOFT_CAP))
    return capped, jnp.where(allowed, jnp.exp2(SOFT_CAP * LOG2_E * capped), 0.0)


def stats_kernel(place_ref, lengths_ref, kv_ref, slot0, slot1, slot2, slot3, stats_ref, rows_ref):
    join_rows((slot0, slot1, slot2, slot3), rows_ref)
    start, pos, low, high = query_bounds(place_ref, lengths_ref)

    def step(block, carry):
        kv_rows = kv_ref[pl.ds(block * PAIR, PAIR)].reshape(PAIR * CHUNK, 2 * WIDTH)
        sums = [[] for _ in range(4)]
        for first in range(0, SPAN, TILE):
            part = slice(first, first + TILE)
            allowed = allowed_pairs(place_ref, block, start[:, part], pos[:, part])
            for head in range(2):
                query = rows_ref[part, head * WIDTH:(head + 1) * WIDTH]
                grad = rows_ref[part, (2 + head) * WIDTH:(3 + head) * WIDTH]
                _, weights = weighted(kv_rows[:, :WIDTH], query, allowed)
                grad_prob = dot(kv_rows[:, WIDTH:], grad, NT)
                sums[2 * head].append(jnp.sum(weights, axis=0, keepdims=True))
                sums[2 * head + 1].append(jnp.sum(weights * grad_prob, axis=0, keepdims=True))
        return tuple(total + jnp.concatenate(parts, axis=1) for total, parts in zip(carry, sums))

    empty = jnp.zeros((1, SPAN), F32)
    totals = lax.fori_loop(low, high, step, (empty,) * 4)
    stats_ref[...] = jnp.concatenate(totals, axis=0)


def grads_kernel(
    place_ref, lengths_ref, stats_ref, kv_ref, slot0, slot1, slot2, slot3, query_ref, kv_out_ref, rows_ref, sums_ref
):
    join_rows((slot0, slot1, slot2, slot3), rows_ref)
    start, pos, low, high = query_bounds(place_ref, lengths_ref)
    own = place_ref[1]
    lanes = [stats_ref[own ^ lane] for lane in range(GROUP)]
    stats = jnp.concatenate(
        [
            sum(lanes[lane][:, (slot ^ lane) * CHUNK:((slot ^ lane) + 1) * CHUNK] for lane in range(GROUP))
            for slot in range(GROUP)
        ],
        axis=1,
    )
    inverse = [1.0 / stats[2 * head:2 * head + 1] for head in range(2)]
    deltas = [stats[2 * head + 1:2 * head + 2] * inverse[head] for head in range(2)]
    sums_ref[...] = jnp.zeros_like(sums_ref)

    def clear(block, carry):
        kv_out_ref[pl.ds(block * PAIR, PAIR)] = jnp.zeros((PAIR, CHUNK, 2 * WIDTH), BF16)
        return carry

    lax.fori_loop(0, low, clear, 0)
    lax.fori_loop(high, BLOCKS // PAIR, clear, 0)

    def step(block, carry):
        kv_rows = kv_ref[pl.ds(block * PAIR, PAIR)].reshape(PAIR * CHUNK, 2 * WIDTH)
        key_rows = kv_rows[:, :WIDTH]
        key_sum = jnp.zeros((PAIR * CHUNK, WIDTH), F32)
        value_sum = jnp.zeros((PAIR * CHUNK, WIDTH), F32)
        for first in range(0, SPAN, TILE):
            part = slice(first, first + TILE)
            allowed = allowed_pairs(place_ref, block, start[:, part], pos[:, part])
            for head in range(2):
                query = rows_ref[part, head * WIDTH:(head + 1) * WIDTH]
                grad = rows_ref[part, (2 + head) * WIDTH:(3 + head) * WIDTH]
                capped, weights = weighted(key_rows, query, allowed)
                probs = weights * inverse[head][:, part]
                grad_prob = dot(kv_rows[:, WIDTH:], grad, NT)
                slope = probs * (grad_prob - deltas[head][:, part]) * (QUERY_SCALE - QUERY_SCALE * capped * capped)
                slope = slope.astype(BF16)
                key_sum = key_sum + dot(slope, query, NN)
                value_sum = value_sum + dot(probs.astype(BF16), grad, NN)
                sums_ref[head * WIDTH:(head + 1) * WIDTH, part] += dot(key_rows, slope, TN)
        result = jnp.concatenate([key_sum, value_sum], axis=1).astype(BF16)
        kv_out_ref[pl.ds(block * PAIR, PAIR)] = result.reshape(PAIR, CHUNK, 2 * WIDTH)
        return carry

    lax.fori_loop(low, high, step, 0)
    for slot in range(GROUP):
        query_ref[slot] = sums_ref[:, slot * CHUNK:(slot + 1) * CHUNK].astype(BF16)


def term_kernel(place_ref, wq_ref, wk_ref, wv_ref, query_ref, kv_ref, out_ref):
    rows = wq_ref.shape[0] // 8
    key_part = kv_ref[:, :WIDTH].T
    value_part = kv_ref[:, WIDTH:].T
    for side in range(2):
        for line in range(GROUP):
            block = pl.ds(pl.multiple_of(((place_ref[1] ^ line) * 2 + (place_ref[3] ^ (1 - side))) * rows, 32), rows)
            total = dot(wq_ref[block, :], query_ref[...], NN)
            total = total + dot(wk_ref[block, :], key_part, NN)
            total = total + dot(wv_ref[block, :], value_part, NN)
            out_ref[side, line] = total.astype(BF16)


def run_kernel(body, shapes, scratch, flops, scalars, operands):
    smem = pl.BlockSpec(memory_space=pltpu.SMEM)
    vmem = pl.BlockSpec(memory_space=pltpu.VMEM)
    return pl.pallas_call(
        body,
        out_shape=shapes,
        in_specs=[smem] * len(scalars) + [vmem] * len(operands),
        out_specs=jax.tree.map(lambda _: vmem, shapes),
        scratch_shapes=scratch,
        compiler_params=pltpu.CompilerParams(vmem_limit_bytes=16 * 1024 * 1024),
        cost_estimate=pl.CostEstimate(flops=flops, bytes_accessed=4000000, transcendentals=2000000),
    )(*scalars, *operands)


def shards(inputs, queries, keys, values, grad_out, w_query, w_key, w_value, doc_lengths):
    zh, zl, core = lax.axis_index("zh"), lax.axis_index("zl"), lax.axis_index("c")
    place = jnp.stack([lax.axis_index(PLANE), zl, zh, core]).astype(jnp.int32)
    lengths = doc_lengths.astype(jnp.int32)

    packed = swapped(jnp.concatenate([keys, values, queries, grad_out], axis=1))
    features = lax.all_gather(inputs.T, ("zl", "c"), axis=0, tiled=True)
    packed, features = lax.optimization_barrier((packed, features))
    kv_all = spread(packed[:, :2 * WIDTH], BLOCKS, PLANE)
    rows = gathered(packed[:, 2 * WIDTH:], "zl")
    joined = pltpu.VMEM((SPAN, 4 * WIDTH), BF16)
    stats = run_kernel(
        stats_kernel, jax.ShapeDtypeStruct((4, SPAN), F32), [joined], 500000000, (place, lengths), (kv_all, *rows)
    )
    stats_all = spread(stats, GROUP, "zl")
    query_parts, kv_parts = run_kernel(
        grads_kernel,
        (jax.ShapeDtypeStruct((GROUP, 2 * WIDTH, CHUNK), BF16), jax.ShapeDtypeStruct((BLOCKS, CHUNK, 2 * WIDTH), BF16)),
        [joined, pltpu.VMEM((2 * WIDTH, SPAN), F32)],
        1200000000,
        (place, lengths),
        (stats_all, kv_all, *rows),
    )
    kv_parts = exchange(kv_parts, PLANE)
    query_parts = returned([query_parts[slot] for slot in range(GROUP)], "zl")
    grad_query = swapped(sum(part.astype(F32) for part in query_parts).astype(BF16))
    grad_kv = added(kv_parts).astype(BF16)

    grad_kv = swapped(grad_kv)

    weight = dot(features, grad_kv, NN).astype(BF16).reshape(BLOCKS, -1, 2 * WIDTH)
    weight = added(exchange(weight, PLANE)).astype(BF16).reshape(GROUP, -1, 2 * WIDTH)
    weight = added(exchange(weight, "zh"))

    side = jax.ShapeDtypeStruct((2, GROUP, w_query.shape[0] // 8, CHUNK), BF16)
    terms = run_kernel(term_kernel, side, [], 300000000, (place,), (w_query, w_key, w_value, grad_query, grad_kv))
    both = (terms[1].astype(F32) + partner(terms[0], "c", 1).astype(F32)).astype(BF16)
    pieces = returned([both[slot] for slot in range(GROUP)], "zl")
    grad_input = sum(piece.astype(F32) for piece in pieces).T.astype(BF16)
    return grad_input, weight[:, :WIDTH], weight[:, WIDTH:]


def solution(mesh):
    fine = Mesh(mesh.devices.reshape(4, 4, 4, 4, 2), ("y", "x", "zh", "zl", "c"))
    ctx, head = ("y", "x", "zh"), ("zl", "c")
    split = P(ctx, head)
    return jax.shard_map(
        shards,
        mesh=fine,
        in_specs=(split,) * 5 + (P(None, head),) * 3 + (P(),),
        out_specs=(split,) * 3,
        check_vma=False,
    )
```

```python
import jax
import jax.numpy as jnp
from jax import lax
from jax.experimental import pallas as pl
from jax.experimental.pallas import tpu as pltpu
from jax.sharding import Mesh, PartitionSpec as P

QUERY_SCALE = 1.0 / 12.0
SOFT_CAP = 50.0
LOG2_E = 1.4426950408889634
PLANE = ("y", "x")
LINES = ("zh", "zl")
CHUNK = 128
WIDTH = 128
GROUP = 4
BLOCKS = 16
SPAN = GROUP * CHUNK
PAIR = 2
TILE = 256
NT = (((1,), (1,)), ((), ()))
TN = (((0,), (0,)), ((), ()))
NN = (((1,), (0,)), ((), ()))
F32 = jnp.float32
BF16 = jnp.bfloat16


def dot(left, right, dims):
    return lax.dot_general(left, right, dims, preferred_element_type=F32)


def swapped(value):
    return lax.ppermute(value, LINES, [(a * 4 + b, b * 4 + a) for a in range(4) for b in range(4)])


def partner(value, axis, mask):
    return lax.ppermute(value, axis, [(i, i ^ mask) for i in range(lax.axis_size(axis))])


def gathered(value, axis):
    return [value] + [partner(value, axis, mask) for mask in (1, 2, 3)]


def returned(parts, axis):
    return [parts[0]] + [partner(parts[mask], axis, mask) for mask in (1, 2, 3)]


def exchange(parts, axes):
    return lax.all_to_all(parts, axes, 0, 0, tiled=True)


def spread(value, count, axes):
    return exchange(jnp.broadcast_to(value[None], (count,) + value.shape), axes)


def added(parts):
    return jnp.sum(parts.astype(F32), axis=0)


def query_bounds(place_ref, lengths_ref):
    block, own = place_ref[0], place_ref[1]
    first = block * SPAN
    lane = lax.broadcasted_iota(jnp.int32, (1, CHUNK), 1)
    pos = jnp.concatenate([first + (own ^ slot) * CHUNK + lane for slot in range(GROUP)], axis=1)
    start = jnp.zeros((1, SPAN), jnp.int32)
    end = jnp.int32(0)
    earliest = jnp.int32(0)
    for doc in range(lengths_ref.shape[0]):
        end = end + lengths_ref[doc]
        start = jnp.where(pos >= end, end, start)
        earliest = jnp.where(end <= first, end, earliest)
    return start, pos, lax.div(earliest, PAIR * SPAN), lax.div(block, PAIR) + 1


def join_rows(slots, rows_ref):
    for slot in range(GROUP):
        rows_ref[slot * CHUNK:(slot + 1) * CHUNK, :] = slots[slot][...]


def allowed_pairs(place_ref, block, start, pos):
    row = lax.broadcasted_iota(jnp.int32, (PAIR * CHUNK, TILE), 0)
    key_pos = (block * PAIR) * SPAN + place_ref[1] * CHUNK + row + jnp.where(row >= CHUNK, SPAN - CHUNK, 0)
    return (key_pos >= start) & (key_pos <= pos)


def weighted(key_rows, query, allowed):
    capped = jnp.tanh(dot(key_rows, query, NT) * (QUERY_SCALE / SOFT_CAP))
    return capped, jnp.where(allowed, jnp.exp2(SOFT_CAP * LOG2_E * capped), 0.0)


def stats_kernel(place_ref, lengths_ref, kv_ref, slot0, slot1, slot2, slot3, stats_ref, rows_ref):
    join_rows((slot0, slot1, slot2, slot3), rows_ref)
    start, pos, low, high = query_bounds(place_ref, lengths_ref)

    def step(block, carry):
        kv_rows = kv_ref[pl.ds(block * PAIR, PAIR)].reshape(PAIR * CHUNK, 2 * WIDTH)
        sums = [[] for _ in range(4)]
        for first in range(0, SPAN, TILE):
            part = slice(first, first + TILE)
            allowed = allowed_pairs(place_ref, block, start[:, part], pos[:, part])
            for head in range(2):
                query = rows_ref[part, head * WIDTH:(head + 1) * WIDTH]
                grad = rows_ref[part, (2 + head) * WIDTH:(3 + head) * WIDTH]
                _, weights = weighted(kv_rows[:, :WIDTH], query, allowed)
                grad_prob = dot(kv_rows[:, WIDTH:], grad, NT)
                sums[2 * head].append(jnp.sum(weights, axis=0, keepdims=True))
                sums[2 * head + 1].append(jnp.sum(weights * grad_prob, axis=0, keepdims=True))
        return tuple(total + jnp.concatenate(parts, axis=1) for total, parts in zip(carry, sums))

    empty = jnp.zeros((1, SPAN), F32)
    totals = lax.fori_loop(low, high, step, (empty,) * 4)
    stats_ref[...] = jnp.concatenate(totals, axis=0)


def grads_kernel(
    place_ref, lengths_ref, stats_ref, kv_ref, slot0, slot1, slot2, slot3, query_ref, kv_out_ref, rows_ref, sums_ref
):
    join_rows((slot0, slot1, slot2, slot3), rows_ref)
    start, pos, low, high = query_bounds(place_ref, lengths_ref)
    own = place_ref[1]
    lanes = [stats_ref[own ^ lane] for lane in range(GROUP)]
    stats = jnp.concatenate(
        [
            sum(lanes[lane][:, (slot ^ lane) * CHUNK:((slot ^ lane) + 1) * CHUNK] for lane in range(GROUP))
            for slot in range(GROUP)
        ],
        axis=1,
    )
    inverse = [1.0 / stats[2 * head:2 * head + 1] for head in range(2)]
    deltas = [stats[2 * head + 1:2 * head + 2] * inverse[head] for head in range(2)]
    sums_ref[...] = jnp.zeros_like(sums_ref)

    def clear(block, carry):
        kv_out_ref[pl.ds(block * PAIR, PAIR)] = jnp.zeros((PAIR, CHUNK, 2 * WIDTH), BF16)
        return carry

    lax.fori_loop(0, low, clear, 0)
    lax.fori_loop(high, BLOCKS // PAIR, clear, 0)

    def step(block, carry):
        kv_rows = kv_ref[pl.ds(block * PAIR, PAIR)].reshape(PAIR * CHUNK, 2 * WIDTH)
        key_rows = kv_rows[:, :WIDTH]
        key_sum = jnp.zeros((PAIR * CHUNK, WIDTH), F32)
        value_sum = jnp.zeros((PAIR * CHUNK, WIDTH), F32)
        for first in range(0, SPAN, TILE):
            part = slice(first, first + TILE)
            allowed = allowed_pairs(place_ref, block, start[:, part], pos[:, part])
            for head in range(2):
                query = rows_ref[part, head * WIDTH:(head + 1) * WIDTH]
                grad = rows_ref[part, (2 + head) * WIDTH:(3 + head) * WIDTH]
                capped, weights = weighted(key_rows, query, allowed)
                probs = weights * inverse[head][:, part]
                grad_prob = dot(kv_rows[:, WIDTH:], grad, NT)
                slope = probs * (grad_prob - deltas[head][:, part]) * (QUERY_SCALE - QUERY_SCALE * capped * capped)
                slope = slope.astype(BF16)
                key_sum = key_sum + dot(slope, query, NN)
                value_sum = value_sum + dot(probs.astype(BF16), grad, NN)
                sums_ref[head * WIDTH:(head + 1) * WIDTH, part] += dot(key_rows, slope, TN)
        result = jnp.concatenate([key_sum, value_sum], axis=1).astype(BF16)
        kv_out_ref[pl.ds(block * PAIR, PAIR)] = result.reshape(PAIR, CHUNK, 2 * WIDTH)
        return carry

    lax.fori_loop(low, high, step, 0)
    for slot in range(GROUP):
        query_ref[slot] = sums_ref[:, slot * CHUNK:(slot + 1) * CHUNK].astype(BF16)


def term_kernel(place_ref, wq_ref, wk_ref, wv_ref, query_ref, kv_ref, out_ref):
    rows = wq_ref.shape[0] // 8
    key_part = kv_ref[:, :WIDTH].T
    value_part = kv_ref[:, WIDTH:].T
    for side in range(2):
        for line in range(GROUP):
            block = pl.ds(pl.multiple_of(((place_ref[1] ^ line) * 2 + (place_ref[3] ^ (1 - side))) * rows, 32), rows)
            total = dot(wq_ref[block, :], query_ref[...], NN)
            total = total + dot(wk_ref[block, :], key_part, NN)
            total = total + dot(wv_ref[block, :], value_part, NN)
            out_ref[side, line] = total.astype(BF16)


def run_kernel(body, shapes, scratch, flops, scalars, operands):
    smem = pl.BlockSpec(memory_space=pltpu.SMEM)
    vmem = pl.BlockSpec(memory_space=pltpu.VMEM)
    return pl.pallas_call(
        body,
        out_shape=shapes,
        in_specs=[smem] * len(scalars) + [vmem] * len(operands),
        out_specs=jax.tree.map(lambda _: vmem, shapes),
        scratch_shapes=scratch,
        compiler_params=pltpu.CompilerParams(vmem_limit_bytes=16 * 1024 * 1024),
        cost_estimate=pl.CostEstimate(flops=flops, bytes_accessed=4000000, transcendentals=2000000),
    )(*scalars, *operands)


def shards(inputs, queries, keys, values, grad_out, w_query, w_key, w_value, doc_lengths):
    zh, zl, core = lax.axis_index("zh"), lax.axis_index("zl"), lax.axis_index("c")
    place = jnp.stack([lax.axis_index(PLANE), zl, zh, core]).astype(jnp.int32)
    lengths = doc_lengths.astype(jnp.int32)

    packed = swapped(jnp.concatenate([keys, values, queries, grad_out], axis=1))
    features = lax.all_gather(inputs.T, ("zl", "c"), axis=0, tiled=True)
    packed, features = lax.optimization_barrier((packed, features))
    kv_all = spread(packed[:, :2 * WIDTH], BLOCKS, PLANE)
    rows = gathered(packed[:, 2 * WIDTH:], "zl")
    joined = pltpu.VMEM((SPAN, 4 * WIDTH), BF16)
    stats = run_kernel(
        stats_kernel, jax.ShapeDtypeStruct((4, SPAN), F32), [joined], 500000000, (place, lengths), (kv_all, *rows)
    )
    stats_all = spread(stats, GROUP, "zl")
    query_parts, kv_parts = run_kernel(
        grads_kernel,
        (jax.ShapeDtypeStruct((GROUP, 2 * WIDTH, CHUNK), BF16), jax.ShapeDtypeStruct((BLOCKS, CHUNK, 2 * WIDTH), BF16)),
        [joined, pltpu.VMEM((2 * WIDTH, SPAN), F32)],
        1200000000,
        (place, lengths),
        (stats_all, kv_all, *rows),
    )
    kv_parts = exchange(kv_parts, PLANE)
    query_parts = returned([query_parts[slot] for slot in range(GROUP)], "zl")
    grad_query = sum(part.astype(F32) for part in query_parts).astype(BF16)
    grad_kv = added(kv_parts).astype(BF16)

    grad_kv = swapped(grad_kv)

    weight = dot(features, grad_kv, NN).astype(BF16).reshape(BLOCKS, -1, 2 * WIDTH)
    _, grad_query = lax.optimization_barrier((weight, grad_query))
    grad_query = swapped(grad_query)
    weight = added(exchange(weight, PLANE)).astype(BF16).reshape(GROUP, -1, 2 * WIDTH)
    weight = added(exchange(weight, "zh"))

    side = jax.ShapeDtypeStruct((2, GROUP, w_query.shape[0] // 8, CHUNK), BF16)
    terms = run_kernel(term_kernel, side, [], 300000000, (place,), (w_query, w_key, w_value, grad_query, grad_kv))
    both = (terms[1].astype(F32) + partner(terms[0], "c", 1).astype(F32)).astype(BF16)
    pieces = returned([both[slot] for slot in range(GROUP)], "zl")
    grad_input = sum(piece.astype(F32) for piece in pieces).T.astype(BF16)
    return grad_input, weight[:, :WIDTH], weight[:, WIDTH:]


def solution(mesh):
    fine = Mesh(mesh.devices.reshape(4, 4, 4, 4, 2), ("y", "x", "zh", "zl", "c"))
    ctx, head = ("y", "x", "zh"), ("zl", "c")
    split = P(ctx, head)
    return jax.shard_map(
        shards,
        mesh=fine,
        in_specs=(split,) * 5 + (P(None, head),) * 3 + (P(),),
        out_specs=(split,) * 3,
        check_vma=False,
    )
```
